32 devices in a mesh: rep: 2 (over y), ad: 4 (over z), tp: 4 (over x, core).
Axes of the slice: x: 2, y: 2, z: 4, core: 2. Of those that a mesh axis runs over, the one named last changes fastest.
Arguments:
- activations: bfloat16 [4, 1024, 8192], P(None, ('rep', 'ad'), 'tp'), parts along dimension 1, may hold values from -6 to 6
- adapter_ids: int32 [4, 1024], P(None, ('rep', 'ad')), parts along dimension 1, may hold values from 0 to 127, as said below
- owner_slots: int32 [256], P('rep'), parts along dimension 0, may hold values from 0 to 127, as said below
- base_weight: bfloat16 [8192, 8192], P(None, 'tp'), may hold values from -0.0625 to 0.0625
- shrink_weight: bfloat16 [256, 8192, 64], P(('rep', 'ad'), 'tp'), parts along dimension 0, may hold values from -0.0625 to 0.0625
- expand_weight: bfloat16 [256, 64, 8192], P(('rep', 'ad'), None, 'tp'), parts along dimension 0, may hold values from -0.75 to 0.75
Outputs:
- result: bfloat16 [4, 1024, 8192], P(None, ('rep', 'ad'), 'tp'), parts along dimension 1
The draws below stay inside these ranges and needn't reach their ends.
There are 2 independent parts, one for each index of `rep`. The reference program is written for one: setup_inputs(seed, part) draws one part's arguments, and reference() takes and returns one part's arrays. A program takes and returns all parts, laid end to end along the dimension named above; an argument that names none is the same for every part. Nothing has to cross between parts.
Inputs may be any that keep to these rules, and one draw needn't show every extreme that they name: `owner_slots`: A permutation: each entry of the stacked adapter arrays belongs to exactly one adapter. `adapter_ids`: of the 128 rows that one index of ad holds in one step, at most 64 have a slot in the block of entries stored by one index of ad (slot // 32); some index of ad reaches 64 in every step.
All inputs are finite; a program needn't handle non-finite values.
Results may differ from the reference program's by a relative error of at most 0.005.
Values may be sent and summed in bfloat16 or wider, within the bound.
A program may use at most 192 MiB of HBM per device.

```python
import jax
import jax.numpy as jnp
from jax import lax

D = 8192
RANK = 64
STEPS = 4
ROW_DEV = 128
ADP_DEV = 32
ROWS = 512
ADAPTERS = 128


def shared_order(key):
    return jax.random.permutation(key, ADAPTERS).astype(jnp.int32)


def draw_owner_slots(key, part):
    return shared_order(key)


def draw_adapter_ids(key, part):
    permuted = shared_order(key)
    key = jax.random.fold_in(key, 7)
    key_shared, key_each, key_others, key_shuffle, key_local = jax.random.split(key, 5)
    groups = ADAPTERS // ADP_DEV
    capacity = ROW_DEV // 2
    shape = (STEPS, groups, ROW_DEV)
    hot_shared = jax.random.randint(key_shared, (STEPS, 1, 1), 0, groups)
    hot_each = jax.random.randint(key_each, (STEPS, groups, 1), 0, groups)
    step_index = jnp.arange(STEPS)[:, None, None]
    hot_group = jnp.where(step_index == 0, hot_shared, hot_each)
    others = (hot_group + 1 + jax.random.randint(key_others, shape, 0, groups - 1)) % groups
    lane_index = jnp.arange(ROW_DEV)[None, None, :]
    owner_group = jnp.where(lane_index < capacity, hot_group, others)
    scores = jax.random.randint(key_shuffle, shape, 0, 2 ** 20) * ROW_DEV + lane_index
    shuffle = jnp.argsort(scores, axis=-1)
    owner_group = jnp.take_along_axis(owner_group, shuffle, axis=-1)
    local_index = jax.random.randint(key_local, shape, 0, ADP_DEV)
    slot_index = owner_group * ADP_DEV + local_index
    inverse = jnp.zeros((ADAPTERS,), jnp.int32).at[permuted].set(jnp.arange(ADAPTERS, dtype=jnp.int32))
    return inverse[slot_index].reshape(STEPS, ROWS).astype(jnp.int32)


def level_of(stream_key, shape, shards, least, top_value):
    def one(position, parts):
        heights = jax.random.uniform(jax.random.fold_in(jax.random.fold_in(stream_key, 6), position), (parts,), jnp.float32, least / len(shards), top_value / len(shards))
        return jnp.repeat(jnp.exp(heights), shape[position] // parts).reshape((-1,) + (1,) * (len(shape) - position - 1))

    gain = one(*shards[0])
    for cut in shards[1:]:
        gain = gain * one(*cut)
    return gain


def normal_values(stream_key, dims, spread, limit, shards=(), kind=jnp.bfloat16):
    entries = jax.random.normal(stream_key, dims, jnp.float32) * spread
    if len(shards) > 0:
        entries = level_of(stream_key, dims, shards, -0.22, 0.18) * entries
    return jnp.clip(entries, min=-limit, max=limit).astype(kind)


def setup_inputs(seed: int = 0, part: int = 0) -> dict:
    key_list = jax.random.split(jax.random.key(seed), 7)
    own_keys = jax.random.split(jax.random.fold_in(key_list[6], part), 7)
    activations = normal_values(own_keys[0], (STEPS, ROWS, D), 1.0, 6.0, ((1, 4), (2, 4)))
    adapter_ids = draw_adapter_ids(jax.random.fold_in(jax.random.fold_in(key_list[6], part), 71), part)
    owner_slots = draw_owner_slots(jax.random.fold_in(jax.random.fold_in(key_list[6], part), 71), part)
    base_weight = normal_values(key_list[3], (D, D), D ** -0.5, 0.0625, ((1, 4),))
    shrink_weight = normal_values(own_keys[4], (ADAPTERS, D, RANK), D ** -0.5, 0.0625, ((0, 4), (1, 4)))
    expand_weight = normal_values(own_keys[5], (ADAPTERS, RANK, D), RANK ** -0.5, 0.75, ((0, 4), (2, 4)))
    return {"activations": activations, "adapter_ids": adapter_ids, "owner_slots": owner_slots, "base_weight": base_weight, "shrink_weight": shrink_weight, "expand_weight": expand_weight}


def reference(activations, adapter_ids, owner_slots, base_weight, shrink_weight, expand_weight):
    flat_rows = activations.reshape(STEPS * ROWS, D)
    flat_ids = adapter_ids.reshape(STEPS * ROWS)
    base_out = jnp.dot(flat_rows, base_weight, preferred_element_type=jnp.float32)
    row_slots = owner_slots[flat_ids].astype(jnp.int32)
    blocks = 16

    def block_fn(items):
        rows_block, slot_block = items
        shrink_rows = shrink_weight[slot_block].astype(jnp.float32)
        low_rank = jnp.einsum('rd,rdk->rk', rows_block.astype(jnp.float32), shrink_rows).astype(jnp.bfloat16)
        expand_rows = expand_weight[slot_block].astype(jnp.float32)
        return jnp.einsum('rk,rkd->rd', low_rank.astype(jnp.float32), expand_rows).astype(jnp.bfloat16)

    delta_rows = lax.map(block_fn, (flat_rows.reshape(-1, blocks, D), row_slots.reshape(-1, blocks)))
    delta_rows = delta_rows.reshape(STEPS * ROWS, D)
    result = (base_out + delta_rows.astype(jnp.float32)).astype(jnp.bfloat16)
    return result.reshape(STEPS, ROWS, D)
```

```python
import jax
import jax.numpy as jnp
from jax import lax
from jax.sharding import PartitionSpec as P


def row_places(slots, adp_dev):
    row_count = slots.shape[-1]
    owner = slots // adp_dev
    index = jnp.arange(row_count, dtype=jnp.int32)
    before = index[None, :] < index[:, None]
    same = owner[..., :, None] == owner[..., None, :]
    place = jnp.sum((same & before).astype(jnp.int32), axis=-1)
    return owner, place


def sum_over_tp(value):
    size = lax.axis_size("tp")
    stride = 1
    while stride < size:
        pairs = [(i, i ^ stride) for i in range(size)]
        value = value + lax.ppermute(value, "tp", pairs)
        stride *= 2
    return value


def body(activations, adapter_ids, owner_slots, base_weight, shrink_weight, expand_weight):
    steps, row_count, width = activations.shape
    adp_dev, _, rank = shrink_weight.shape
    columns = base_weight.shape[1]
    groups = lax.axis_size("ad")
    me = lax.axis_index("ad")
    capacity = row_count // 2

    matches = adapter_ids[..., None] == jnp.arange(owner_slots.shape[0], dtype=jnp.int32)
    slots = jnp.sum(jnp.where(matches, owner_slots, 0), axis=-1)
    owner, place = row_places(slots, adp_dev)
    target = owner * capacity + place
    places = (
        target[:, None, :] == jnp.arange(groups * capacity, dtype=jnp.int32)[None, :, None]
    ).astype(jnp.bfloat16)

    every_slot = lax.all_gather(slots, "ad")
    every_owner, every_place = row_places(every_slot, adp_dev)
    here = jnp.where(every_owner == me, every_place, -1)
    hit = here[:, :, None, :] == jnp.arange(capacity, dtype=jnp.int32)[:, None]
    local = jnp.sum(jnp.where(hit, (every_slot % adp_dev + 1)[:, :, None, :], 0), axis=-1) - 1

    received = []
    for s in range(steps):
        send = jnp.dot(
            places[s], activations[s], preferred_element_type=jnp.float32
        ).astype(jnp.bfloat16)
        send = send.reshape(groups, capacity, width)
        received.append(lax.all_to_all(send, "ad", split_axis=0, concat_axis=0, tiled=True))

    gathered = lax.all_gather(
        activations.reshape(steps * row_count, width), "tp", axis=1, tiled=True
    )
    base_out = jnp.dot(gathered, base_weight, preferred_element_type=jnp.float32)
    base_out = base_out.reshape(steps, row_count, columns)

    down = shrink_weight.transpose(1, 0, 2).reshape(width, adp_dev * rank)
    up = expand_weight.reshape(adp_dev * rank, columns)
    outs = []
    for s in range(steps):
        rows = received[s].reshape(groups * capacity, width)
        mark = local[:, s].reshape(groups * capacity, 1) == jnp.arange(adp_dev, dtype=jnp.int32)
        every = jnp.dot(rows, down, preferred_element_type=jnp.float32)
        every = every.reshape(groups * capacity, adp_dev, rank)
        partial = jnp.sum(jnp.where(mark[..., None], every, 0.0), axis=1)
        low_rank = sum_over_tp(partial).astype(jnp.bfloat16)
        spread = jnp.where(mark[..., None], low_rank[:, None, :], jnp.zeros((), jnp.bfloat16))
        delta = jnp.dot(
            spread.reshape(groups * capacity, adp_dev * rank),
            up,
            preferred_element_type=jnp.float32,
        ).astype(jnp.bfloat16)
        returned = lax.all_to_all(
            delta.reshape(groups, capacity, columns), "ad", split_axis=0, concat_axis=0, tiled=True
        )
        back = jnp.einsum(
            "cr,cf->rf",
            places[s],
            returned.reshape(groups * capacity, columns),
            preferred_element_type=jnp.float32,
        )
        outs.append((base_out[s] + back).astype(jnp.bfloat16))
    return jnp.stack(outs)


def solution(mesh):
    in_specs = (
        P(None, ("rep", "ad"), "tp"),
        P(None, ("rep", "ad")),
        P("rep"),
        P(None, "tp"),
        P(("rep", "ad"), "tp", None),
        P(("rep", "ad"), None, "tp"),
    )
    out_specs = P(None, ("rep", "ad"), "tp")
    return jax.shard_map(body, mesh=mesh, in_specs=in_specs, out_specs=out_specs, check_vma=False)
```

```python
import jax
import jax.numpy as jnp
from jax import lax
from jax.sharding import PartitionSpec as P


def row_places(slots, adp_dev):
    row_count = slots.shape[-1]
    owner = slots // adp_dev
    index = jnp.arange(row_count, dtype=jnp.int32)
    before = index[None, :] < index[:, None]
    same = owner[..., :, None] == owner[..., None, :]
    place = jnp.sum((same & before).astype(jnp.int32), axis=-1)
    return owner, place


def sum_over_tp(value):
    size = lax.axis_size("tp")
    stride = 1
    while stride < size:
        pairs = [(i, i ^ stride) for i in range(size)]
        value = value + lax.ppermute(value, "tp", pairs)
        stride *= 2
    return value


def body(activations, adapter_ids, owner_slots, base_weight, shrink_weight, expand_weight):
    steps, row_count, width = activations.shape
    adp_dev, _, rank = shrink_weight.shape
    columns = base_weight.shape[1]
    groups = lax.axis_size("ad")
    me = lax.axis_index("ad")
    capacity = row_count // 2

    matches = adapter_ids[..., None] == jnp.arange(owner_slots.shape[0], dtype=jnp.int32)
    slots = jnp.sum(jnp.where(matches, owner_slots, 0), axis=-1)
    owner, place = row_places(slots, adp_dev)
    target = lax.rem(owner - me + groups, groups) * capacity + place
    hit = target[:, None, :] == jnp.arange(groups * capacity, dtype=jnp.int32)[None, :, None]
    places = hit.astype(jnp.bfloat16)
    marks = jnp.sum(jnp.where(hit, (slots % adp_dev + 1)[:, None, :], 0), axis=-1) - 1
    marks = marks.reshape(steps, groups, capacity)

    def shifted(block, k):
        if k % groups == 0:
            return block
        return lax.ppermute(block, "ad", [(i, (i + k) % groups) for i in range(groups)])

    local = jnp.stack([shifted(marks[:, k], k) for k in range(groups)], axis=1)

    received = []
    for s in range(steps):
        send = jnp.dot(
            places[s], activations[s], preferred_element_type=jnp.float32
        ).astype(jnp.bfloat16)
        send = send.reshape(groups, capacity, width)
        received.append(jnp.concatenate([shifted(send[k], k) for k in range(groups)]))

    gathered = lax.all_gather(
        activations.reshape(steps * row_count, width), "tp", axis=1, tiled=True
    )
    base_out = jnp.dot(gathered, base_weight, preferred_element_type=jnp.float32)
    base_out = base_out.reshape(steps, row_count, columns)

    down = shrink_weight.transpose(1, 0, 2).reshape(width, adp_dev * rank)
    up = expand_weight.reshape(adp_dev * rank, columns)
    outs = []
    for s in range(steps):
        rows = received[s]
        mark = local[s].reshape(groups * capacity, 1) == jnp.arange(adp_dev, dtype=jnp.int32)
        every = jnp.dot(rows, down, preferred_element_type=jnp.float32)
        every = every.reshape(groups * capacity, adp_dev, rank)
        partial = jnp.sum(jnp.where(mark[..., None], every, 0.0), axis=1)
        low_rank = sum_over_tp(partial).astype(jnp.bfloat16)
        spread = jnp.where(mark[..., None], low_rank[:, None, :], jnp.zeros((), jnp.bfloat16))
        delta = jnp.dot(
            spread.reshape(groups * capacity, adp_dev * rank),
            up,
            preferred_element_type=jnp.float32,
        ).astype(jnp.bfloat16)
        delta = delta.reshape(groups, capacity, columns)
        returned = jnp.concatenate([shifted(delta[k], groups - k) for k in range(groups)])
        back = jnp.einsum(
            "cr,cf->rf",
            places[s],
            returned,
            preferred_element_type=jnp.float32,
        )
        outs.append((base_out[s] + back).astype(jnp.bfloat16))
    return jnp.stack(outs)


def solution(mesh):
    in_specs = (
        P(None, ("rep", "ad"), "tp"),
        P(None, ("rep", "ad")),
        P("rep"),
        P(None, "tp"),
        P(("rep", "ad"), "tp", None),
        P(("rep", "ad"), None, "tp"),
    )
    out_specs = P(None, ("rep", "ad"), "tp")
    return jax.shard_map(body, mesh=mesh, in_specs=in_specs, out_specs=out_specs, check_vma=False)
```

```python
import functools

import jax
import jax.numpy as jnp
from jax import lax
from jax.experimental import pallas as pl
from jax.experimental.pallas import tpu as pltpu
from jax.sharding import PartitionSpec as P


def row_places(slots, adp_dev):
    row_count = slots.shape[-1]
    owner = slots // adp_dev
    index = jnp.arange(row_count, dtype=jnp.int32)
    before = index[None, :] < index[:, None]
    same = owner[..., :, None] == owner[..., None, :]
    place = jnp.sum((same & before).astype(jnp.int32), axis=-1)
    return owner, place


MESH = pl.DeviceIdType.MESH
LANES = 128
TILE = 512


def kernel(
    groups, shards, send_ref, act_ref, mark_ref, wide_ref, back_ref, base_ref, down_ref, up_ref,
    out_ref, rows, acts, total, down, up, delta, back, part, parts, tiles,
    row_send, row_recv, act_send, act_recv, part_send, part_recv, back_send, back_recv, load, stream,
):
    steps, count, width = rows.shape
    capacity = count // groups
    columns = up_ref.shape[1]
    inner = up_ref.shape[0]
    me_ad, me_tp = lax.axis_index("ad"), lax.axis_index("tp")

    def on_ad(k):
        return {"ad": lax.rem(me_ad + k + groups, groups)}

    def on_tp(k):
        return {"tp": lax.rem(me_tp + k, shards)}

    def block(k):
        return pl.ds(k * capacity, capacity)

    def remote(src, dst, send_sem, recv_sem, device):
        return pltpu.make_async_remote_copy(
            src_ref=src, dst_ref=dst, send_sem=send_sem, recv_sem=recv_sem,
            device_id=device, device_id_type=MESH,
        )

    def row_copy(s, k):
        return remote(send_ref.at[s, k], rows.at[s, block(k)], row_send.at[s, k],
                      row_recv.at[s, k], on_ad(k))

    def act_copy(k):
        return remote(act_ref, acts.at[k], act_send.at[k], act_recv.at[k], on_tp(k))

    def part_copy(s, k):
        return remote(part.at[s], parts.at[s, k], part_send.at[s, k], part_recv.at[s, k], on_tp(k))

    def back_copy(s, k):
        return remote(delta.at[s, block(k)], back.at[s, block(k)], back_send.at[s, k],
                      back_recv.at[s, k], on_ad(-k))

    barrier = pltpu.get_barrier_semaphore()
    for k in range(1, groups):
        pl.semaphore_signal(barrier, inc=1, device_id=on_ad(k), device_id_type=MESH)
    for k in range(1, shards):
        pl.semaphore_signal(barrier, inc=1, device_id=on_tp(k), device_id_type=MESH)
    pl.semaphore_wait(barrier, groups + shards - 2)

    for s in range(steps):
        for k in range(1, groups):
            row_copy(s, k).start()
    for k in range(1, shards):
        act_copy(k).start()
    own = [pltpu.make_async_copy(send_ref.at[s, 0], rows.at[s, block(0)], load.at[3 + s])
           for s in range(steps)]
    loads = [
        pltpu.make_async_copy(act_ref, acts.at[0], load.at[0]),
        pltpu.make_async_copy(down_ref, down, load.at[1]),
        pltpu.make_async_copy(up_ref, up, load.at[2]),
    ]
    for copy in loads + own:
        copy.start()

    step_columns = tiles.shape[2]
    per_shard = columns // step_columns

    def add_base(k):
        source = lax.rem(me_tp - k + shards, shards)

        def tile_copy(n):
            return pltpu.make_async_copy(
                base_ref.at[pl.ds(source * width, width), pl.ds(n * step_columns, step_columns)],
                tiles.at[n % 2], stream.at[n % 2],
            )

        tile_copy(0).start()
        for n in range(per_shard):
            if n + 1 < per_shard:
                tile_copy(n + 1).start()
            tile_copy(n).wait()
            where = pl.ds(n * step_columns, step_columns)

            @pl.loop(0, steps)
            def _(s):
                piece = pl.ds(s * row_count, row_count)
                value = jnp.dot(
                    acts[k, piece, :], tiles[n % 2], preferred_element_type=jnp.float32
                )
                if k == 0:
                    total[piece, where] = value
                else:
                    total[piece, where] += value

    row_count = out_ref.shape[1]
    loads[0].wait()
    add_base(0)
    loads[1].wait()

    def shrink(s):
        own[s].wait()
        for k in range(1, groups):
            row_copy(s, k).wait_recv()
        part[s] = jnp.zeros((count, LANES), jnp.float32)

        @pl.loop(0, inner // TILE)
        def _(n):
            where = pl.ds(pl.multiple_of(n * TILE, TILE), TILE)
            every = lax.dot_general(
                rows[s], down[where, :], (((1,), (1,)), ((), ())),
                preferred_element_type=jnp.float32,
            )
            mask = jnp.dot(mark_ref[s], wide_ref[:, where], preferred_element_type=jnp.float32)
            every = jnp.where(mask > 0.5, every, 0.0)
            value = part[s]
            for j in range(TILE // LANES):
                value += every[:, j * LANES:(j + 1) * LANES]
            part[s] = value

        for k in range(1, shards):
            part_copy(s, k).start()

    def expand(s):
        low = part[s]
        for k in range(1, shards):
            part_copy(s, k).wait_recv()
            low += parts[s, k]
        low = low + pltpu.roll(low, LANES // 2, 1)
        low = low.astype(jnp.bfloat16).astype(jnp.float32)
        low = jnp.concatenate([low] * (inner // LANES), axis=1)
        mask = jnp.dot(mark_ref[s], wide_ref[...], preferred_element_type=jnp.float32)
        spread = jnp.where(mask > 0.5, low, 0.0).astype(jnp.bfloat16)
        for n in range(columns // step_columns):
            where = pl.ds(n * step_columns, step_columns)
            value = jnp.dot(
                spread, up[:, where], preferred_element_type=jnp.float32
            ).astype(jnp.bfloat16)
            delta[s, :, where] = value
            back[s, block(0), where] = value[:capacity]
        for k in range(1, groups):
            back_copy(s, k).start()

    for s in range(steps):
        shrink(s)
        if s == 1:
            loads[2].wait()
        if s >= 1:
            expand(s - 1)
    expand(steps - 1)

    for k in range(1, shards):
        act_copy(k).wait_recv()
        add_base(k)

    for s in range(steps):
        for k in range(1, groups):
            back_copy(s, k).wait_recv()
        for n in range(columns // step_columns):
            where = pl.ds(n * step_columns, step_columns)
            value = jnp.dot(back_ref[s], back[s, :, where], preferred_element_type=jnp.float32)
            value += total[pl.ds(s * row_count, row_count), where]
            out_ref[s, :, where] = value.astype(jnp.bfloat16)

    for s in range(steps):
        for k in range(1, groups):
            row_copy(s, k).wait_send()
            back_copy(s, k).wait_send()
        for k in range(1, shards):
            part_copy(s, k).wait_send()
    for k in range(1, shards):
        act_copy(k).wait_send()


def body(activations, adapter_ids, owner_slots, base_weight, shrink_weight, expand_weight):
    steps, row_count, width = activations.shape
    adp_dev, _, rank = shrink_weight.shape
    columns = base_weight.shape[1]
    groups = lax.axis_size("ad")
    me = lax.axis_index("ad")
    capacity = row_count // 2

    matches = adapter_ids[..., None] == jnp.arange(owner_slots.shape[0], dtype=jnp.int32)
    slots = jnp.sum(jnp.where(matches, owner_slots, 0), axis=-1)
    owner, place = row_places(slots, adp_dev)
    target = lax.rem(owner - me + groups, groups) * capacity + place
    hit = target[:, None, :] == jnp.arange(groups * capacity, dtype=jnp.int32)[None, :, None]
    places = hit.astype(jnp.bfloat16)
    marks = jnp.sum(jnp.where(hit, (slots % adp_dev + 1)[:, None, :], 0), axis=-1) - 1
    marks = marks.reshape(steps, groups, capacity)

    def shifted(block, k):
        if k % groups == 0:
            return block
        return lax.ppermute(block, "ad", [(i, (i + k) % groups) for i in range(groups)])

    local = jnp.stack([shifted(marks[:, k], k) for k in range(groups)], axis=1)

    send = jnp.einsum(
        "scr,srf->scf", places, activations, preferred_element_type=jnp.float32
    ).astype(jnp.bfloat16).reshape(steps, groups, capacity, width)
    shards = lax.axis_size("tp")
    count = groups * capacity
    inner = adp_dev * rank
    adapter = jnp.arange(adp_dev, dtype=jnp.int32)
    mark = (local.reshape(steps, count, 1) == adapter).astype(jnp.bfloat16)
    wide = (adapter[:, None] == jnp.arange(inner, dtype=jnp.int32) // rank).astype(jnp.bfloat16)
    anywhere = pl.BlockSpec(memory_space=pl.ANY)
    vmem = pl.BlockSpec(memory_space=pltpu.VMEM)
    dma = pltpu.SemaphoreType.DMA
    tile_columns = min(TILE, columns)
    return pl.pallas_call(
        functools.partial(kernel, groups, shards),
        out_shape=jax.ShapeDtypeStruct((steps, row_count, columns), jnp.bfloat16),
        in_specs=[anywhere, anywhere, vmem, vmem, vmem, anywhere, anywhere, anywhere],
        out_specs=vmem,
        scratch_shapes=[
            pltpu.VMEM((steps, count, width), jnp.bfloat16),
            pltpu.VMEM((shards, steps * row_count, width), jnp.bfloat16),
            pltpu.VMEM((steps * row_count, columns), jnp.float32),
            pltpu.VMEM((inner, width), jnp.bfloat16),
            pltpu.VMEM((inner, columns), jnp.bfloat16),
            pltpu.VMEM((steps, count, columns), jnp.bfloat16),
            pltpu.VMEM((steps, count, columns), jnp.bfloat16),
            pltpu.VMEM((steps, count, LANES), jnp.float32),
            pltpu.VMEM((steps, shards, count, LANES), jnp.float32),
            pltpu.VMEM((2, width, tile_columns), jnp.bfloat16),
            dma((steps, groups)),
            dma((steps, groups)),
            dma((shards,)),
            dma((shards,)),
            dma((steps, shards)),
            dma((steps, shards)),
            dma((steps, groups)),
            dma((steps, groups)),
            dma((3 + steps,)),
            dma((2,)),
        ],
        compiler_params=pltpu.CompilerParams(
            collective_id=0, has_side_effects=True, vmem_limit_bytes=60 * 1024 * 1024
        ),
        cost_estimate=pl.CostEstimate(
            flops=2 * steps * (row_count * shards + 2 * count) * inner * width,
            bytes_accessed=2 * (shards * width * columns + 2 * inner * width),
            transcendentals=0,
        ),
    )(
        send,
        activations.reshape(steps * row_count, width),
        mark,
        wide,
        places.transpose(0, 2, 1),
        base_weight,
        shrink_weight.transpose(0, 2, 1).reshape(inner, width),
        expand_weight.reshape(inner, columns),
    )


def solution(mesh):
    in_specs = (
        P(None, ("rep", "ad"), "tp"),
        P(None, ("rep", "ad")),
        P("rep"),
        P(None, "tp"),
        P(("rep", "ad"), "tp", None),
        P(("rep", "ad"), None, "tp"),
    )
    out_specs = P(None, ("rep", "ad"), "tp")
    return jax.shard_map(body, mesh=mesh, in_specs=in_specs, out_specs=out_specs, check_vma=False)
```
